32 devices in a mesh: gr: 4 (over y, x), gc: 8 (over z, core).
Axes of the slice: x: 2, y: 2, z: 4, core: 2. Of those that a mesh axis runs over, the one named last changes fastest.
Arguments:
- phase: bfloat16 [2, 12288, 512], P(None, 'gr', 'gc'), may hold values from -0.59765625 to 0.59765625
- data: bfloat16 [2, 512, 128], P(None, 'gc'), may hold values from -6 to 6
- column_ids: int32 [512], replicated, may hold values from 0 to 8191
- noise_weight: float32 [8192], replicated, may hold values from 0.3 to 3
Outputs:
- fisher: float32 [12288, 12288], P('gr', 'gc')
- dirty_maps: float32 [12288, 128], P(('gr', 'gc'))
The draws below stay inside these ranges and needn't reach their ends.
All inputs are finite; a program needn't handle non-finite values.
Results may differ from the reference program's by a relative error of at most 0.0029.
Values may be sent and summed in bfloat16 or wider, within the bound.
A program may use at most 128 MiB of HBM per device.

```python
import math
import jax
import jax.numpy as jnp
from jax import lax

P_SIZE = 12288
M = 128
SF = 8192
K = 512


def plant(entries, key, low, high):
    extent = entries.shape
    spot = [jax.random.randint(jax.random.fold_in(key, axis), (), 0, extent[axis]) for axis in range(len(extent))]
    entries = entries.at[tuple(spot)].set(low)
    longest = extent.index(max(extent))
    spot[longest] = (spot[longest] + 1) % extent[longest]
    return entries.at[tuple(spot)].set(high)


def strengthened(values, key, source, target, blocks, factor):
    owner, partner = [(jnp.arange(values.shape[dim]) // (values.shape[dim] // blocks)).reshape([-1 if axis == dim else 1 for axis in range(values.ndim)]) for dim in (source, target)]
    chosen = jax.random.permutation(key, blocks)[partner]
    strong = (owner == chosen) | (owner == (partner + blocks // 2) % blocks)
    return jnp.where(strong, factor * values, values)


def level_of(key, dims, pieces, least, high):
    gain = 1.0
    for axis_at, shards_of in pieces:
        steps = jax.random.uniform(jax.random.fold_in(jax.random.fold_in(key, 6), axis_at), (shards_of,), jnp.float32, least / len(pieces), high / len(pieces))
        gain = gain * jnp.repeat(jnp.exp(steps), dims[axis_at] // shards_of).reshape((-1,) + (1,) * (len(dims) - 1 - axis_at))
    return gain


def normal_values(stream_key, extent, deviation, limit, shards=(), kind=jnp.bfloat16):
    entries = deviation * jax.random.normal(stream_key, extent, jnp.float32)
    if shards:
        entries = entries * level_of(stream_key, extent, shards, -0.22, 0.18)
    return jnp.clip(entries, -limit, limit).astype(kind)


def bell_draw_with(rng, extent, scale, most, cuts, heavy, kind=jnp.bfloat16):
    drawn = scale * jax.random.normal(rng, extent, jnp.float32)
    if cuts:
        drawn = drawn * level_of(rng, extent, cuts, -0.22, 0.18)
    return jnp.clip(strengthened(drawn, jax.random.fold_in(rng, 3), *heavy), -most, most).astype(kind)


def setup_inputs(seed: int = 0) -> dict:
    key_of = jax.random.split(jax.random.key(seed), 5)
    phase = bell_draw_with(key_of[0], (2, P_SIZE, K), 0.1, 0.59765625, ((1, 4), (2, 8)), (2, 1, 8, 2.0))
    data = normal_values(key_of[1], (2, K, M), 1.0, 6.0, ((1, 8),))
    column_ids = plant(jax.random.randint(key_of[2], (K,), 0, SF), jax.random.fold_in(key_of[2], 1), 0, SF - 1).astype(jnp.int32)
    noise_weight = jnp.clip(jnp.exp(jax.random.uniform(key_of[3], (SF,), jnp.float32, math.log(0.3), math.log(3.0))), 0.3, 3.0)
    return {"phase": phase, "data": data, "column_ids": column_ids, "noise_weight": noise_weight}


def reference(phase, data, column_ids, noise_weight):
    weight = jnp.take(noise_weight, column_ids.astype(jnp.int32))
    weighted = (phase.astype(jnp.float32) * weight).astype(jnp.bfloat16)
    left_flat = jnp.concatenate([phase[0], phase[1]], axis=1)
    right_flat = jnp.concatenate([weighted[0], weighted[1]], axis=1)
    fisher = lax.dot_general(left_flat, right_flat, (((1,), (1,)), ((), ())), preferred_element_type=jnp.float32)
    data_flat = jnp.concatenate([data[0], data[1]], axis=0)
    dirty_maps = jnp.dot(right_flat, data_flat, preferred_element_type=jnp.float32)
    return fisher, dirty_maps
```

```python
import functools
import math

import jax
import jax.numpy as jnp
from jax import lax
from jax.experimental import pallas as pl
from jax.experimental.pallas import tpu as pltpu
from jax.sharding import PartitionSpec as P

MESH = pl.DeviceIdType.MESH


def gather_kernel(
    G, C, rows, phase_ref, data_ref, left, right, own,
    up_sem, down_sem, twin_sem, root_sem, ring_sem, keep_sem, own_sem, got, got_right,
):
    Z = C // 2
    pixels = phase_ref.shape[1]
    half = phase_ref.shape[2]
    extra = data_ref.shape[0] * data_ref.shape[1]
    Q = right.shape[1]
    parts = Q // rows
    S = 2 * parts
    g, d = lax.axis_index("gr"), lax.axis_index("gc")
    z, c = d // 2, d % 2
    other = 1 - c
    gy, gx = g // 2, g % 2
    pos = (1 - gx) * gy + gx * (G - 1 - gy)
    ry, rx = z // 2, z % 2
    turn = (pos - ((1 - rx) * ry + rx * (G - 1 - ry)) + G) % G
    is_root = turn == 0

    def ring_device(at):
        at = at % G
        far = at // (G // 2)
        return (1 - far) * 2 * at + far * (2 * (G - 1 - at) + 1)

    ahead, behind = ring_device(pos + 1), ring_device(pos + G - 1)
    send_way = (1 - c) * ahead + c * behind
    not_first, not_last = z > 0, z < Z - 1

    barrier = pltpu.get_barrier_semaphore()

    def greet(device):
        pl.semaphore_signal(barrier, inc=1, device_id=device, device_id_type=MESH)

    greet((g, 2 * z + other))
    for core in range(2):
        greet((ahead, 2 * z + core))
        greet((behind, 2 * z + core))

    @pl.when(not_last)
    def _():
        greet((g, d + 2))

    @pl.when(not_first)
    def _():
        greet((g, d - 2))

    pl.semaphore_wait(barrier, 5 + not_last.astype(jnp.int32) + not_first.astype(jnp.int32))

    def remote(src, dst, send_sem, recv_sem, device):
        return pltpu.make_async_remote_copy(
            src_ref=src, dst_ref=dst, send_sem=send_sem, recv_sem=recv_sem, device_id=device, device_id_type=MESH
        )

    def arrived(piece, sem):
        remote(piece, piece, own_sem, sem, (g, d)).wait_recv()

    def spread(src, zb, block, cut, sem):
        dst = left.at[block, cut]

        @pl.when((zb <= z) & not_last)
        def _():
            remote(src, dst, up_sem.at[zb], sem, (g, d + 2)).start()

        @pl.when((zb >= z) & not_first)
        def _():
            remote(src, dst, down_sem.at[zb], sem, (g, d - 2)).start()

        remote(src, dst, twin_sem.at[zb], sem, (g, 2 * z + other)).start()

    def start_of(m):
        return pl.multiple_of((m % 2) * Q + (m // 2) * rows, rows)

    def broadcast(src, zb, block, m):
        at = pl.multiple_of((m // 2) * rows, rows)
        remote(
            src, right.at[block, pl.ds(at, rows)], root_sem.at[zb], got_right.at[block, m // 2],
            (send_way, 2 * z + m % 2),
        ).start()

    def keep(src, block, m):
        at = pl.multiple_of((m // 2) * rows, rows)
        pltpu.make_async_copy(src, right.at[block, pl.ds(at, rows)], keep_sem.at[block]).start()

    tail = pl.ds(pixels, extra)
    own[pl.ds(pixels, half)] = data_ref[0]
    own[pl.ds(pixels + half, half)] = data_ref[1]
    spread(own.at[tail], z, d, tail, got.at[d, S])
    pltpu.make_async_copy(own.at[tail], left.at[d, tail], own_sem).start()

    def step(s, carry):
        @pl.when(s < S)
        def _():
            at = start_of(s)
            cut = pl.ds(at, rows)
            own[cut] = jnp.concatenate([phase_ref[0, cut], phase_ref[1, cut]], axis=1)
            spread(own.at[cut], z, d, cut, got.at[d, s])
            pltpu.make_async_copy(own.at[cut], left.at[d, cut], own_sem).start()

            @pl.when(is_root)
            def _():
                broadcast(own.at[cut], z, d, s)

                @pl.when(s % 2 == c)
                def _():
                    keep(own.at[cut], d, s)

        for zb in range(Z):
            away = jnp.maximum(zb - z, z - zb)
            mine, twin = 2 * zb + c, 2 * zb + other
            m = s - away

            @pl.when((zb != z) & (m >= 0) & (m < S))
            def _():
                cut = pl.ds(start_of(m), rows)
                piece = left.at[mine, cut]
                arrived(piece, got.at[mine, m])
                spread(piece, zb, mine, cut, got.at[mine, m])

                @pl.when(is_root)
                def _():
                    broadcast(piece, zb, mine, m)

                    @pl.when(m % 2 == c)
                    def _():
                        keep(piece, mine, m)

            @pl.when((zb != z) & (s == away))
            def _():
                arrived(left.at[mine, tail], got.at[mine, S])
                spread(left.at[mine, tail], zb, mine, tail, got.at[mine, S])

            n = s - away - 1

            @pl.when((n >= 0) & (n < S))
            def _():
                piece = left.at[twin, pl.ds(start_of(n), rows)]
                arrived(piece, got.at[twin, n])

                @pl.when(is_root & (n % 2 == c))
                def _():
                    keep(piece, twin, n)

            for e in range(2):
                hops = turn if e == 0 else G - turn
                r = s - away - hops

                @pl.when((turn > 0) & (r >= 0) & (r < S) & (r % 2 == c))
                def _():
                    block = 2 * zb + e
                    piece = right.at[block, pl.ds(pl.multiple_of((r // 2) * rows, rows), rows)]
                    arrived(piece, got_right.at[block, r // 2])

                    @pl.when(hops < G - 1)
                    def _():
                        remote(
                            piece, piece, ring_sem.at[block], got_right.at[block, r // 2],
                            (ahead if e == 0 else behind, d),
                        ).start()

        return carry

    lax.fori_loop(0, S + Z - 1 + G, step, 0)

    def sent(piece, sem):
        remote(piece, piece, sem, got.at[0, 0], (g, d)).wait_send()

    for zb in range(Z):
        mine, twin = 2 * zb + c, 2 * zb + other
        arrived(left.at[twin, tail], got.at[twin, S])
        sent(left.at[mine], twin_sem.at[zb])

        @pl.when((zb <= z) & not_last)
        def _():
            sent(left.at[mine], up_sem.at[zb])

        @pl.when((zb >= z) & not_first)
        def _():
            sent(left.at[mine], down_sem.at[zb])

        @pl.when(is_root)
        def _():
            sent(left.at[mine, pl.ds(0, pixels)], root_sem.at[zb])

        for e in range(2):
            block = 2 * zb + e
            hops = turn if e == 0 else G - turn

            @pl.when(is_root)
            def _():
                pltpu.make_async_copy(right.at[block], right.at[block], keep_sem.at[block]).wait()

            @pl.when((turn > 0) & (hops < G - 1))
            def _():
                sent(right.at[block], ring_sem.at[block])

    pltpu.make_async_copy(own, left.at[d], own_sem).wait()


def gather(phase, data, G, C):
    _, pixels, half = phase.shape
    extra = 2 * half
    Z = C // 2
    Q = pixels * G // C
    rows = math.gcd(Q, 192)
    dma = pltpu.SemaphoreType.DMA
    return pl.pallas_call(
        functools.partial(gather_kernel, G, C, rows),
        out_shape=(
            jax.ShapeDtypeStruct((C, pixels + extra, 2 * half), jnp.bfloat16),
            jax.ShapeDtypeStruct((C, Q, 2 * half), jnp.bfloat16),
        ),
        in_specs=[pl.BlockSpec(memory_space=pltpu.VMEM)] * 2,
        out_specs=(pl.BlockSpec(memory_space=pl.ANY),) * 2,
        scratch_shapes=[
            pltpu.VMEM((pixels + extra, 2 * half), jnp.bfloat16),
            dma((Z,)), dma((Z,)), dma((Z,)), dma((Z,)), dma((C,)), dma((C,)), dma,
            dma((C, 2 * (Q // rows) + 1)), dma((C, Q // rows)),
        ],
        compiler_params=pltpu.CompilerParams(
            collective_id=0, has_side_effects=True, vmem_limit_bytes=48 * 2**20
        ),
    )(phase, data)


def product_kernel(where, left, right, own, data, scale, fisher, maps, weighted):
    C = left.shape[0]
    width = left.shape[2]

    def scaled(ref, b):
        return (ref[b].astype(jnp.float32) * scale[b]).astype(jnp.bfloat16)

    @pl.when(pl.program_id(0) == 0)
    def _():
        for b in range(C):
            weighted[:, b * width:(b + 1) * width] = scaled(right, b)

    rows = jnp.concatenate([left[b] for b in range(C)], axis=1)
    fisher[...] = lax.dot_general(
        rows, weighted[...], (((1,), (1,)), ((), ())), preferred_element_type=jnp.float32
    )

    @pl.when(pl.program_id(0) == pl.num_programs(0) - 1)
    def _():
        mine = jnp.concatenate([scaled(own, b) for b in range(C)], axis=1)
        columns = jnp.concatenate([data[b] for b in range(C)], axis=0)
        maps[...] = jnp.dot(mine, columns, preferred_element_type=jnp.float32)


def shards(phase, data, column_ids, noise_weight):
    G, C = lax.axis_size("gr"), lax.axis_size("gc")
    _, pixels, half = phase.shape
    width = 2 * half
    Q = pixels * G // C
    owned = pixels // C
    maps = data.shape[2]
    weight = jnp.take(noise_weight, column_ids).reshape(C, 1, half)
    scale = jnp.concatenate([weight, weight], axis=2)
    left, right = gather(phase, data, G, C)
    tile = math.gcd(pixels, 256)
    once = pl.Buffered(1)
    where = lax.axis_index("gc").astype(jnp.int32).reshape(1)
    return pl.pallas_call(
        product_kernel,
        grid_spec=pltpu.PrefetchScalarGridSpec(
            num_scalar_prefetch=1,
            grid=(pixels // tile,),
            in_specs=[
                pl.BlockSpec((C, tile, width), lambda i, at: (0, i, 0)),
                pl.BlockSpec((C, Q, width), lambda i, at: (0, 0, 0), pipeline_mode=once),
                pl.BlockSpec((C, owned, width), lambda i, at: (0, at[0], 0), pipeline_mode=once),
                pl.BlockSpec((C, width, maps), lambda i, at: (0, pixels // width, 0), pipeline_mode=once),
                pl.BlockSpec((C, 1, width), lambda i, at: (0, 0, 0), pipeline_mode=once),
            ],
            out_specs=[
                pl.BlockSpec((tile, Q), lambda i, at: (i, 0)),
                pl.BlockSpec((owned, maps), lambda i, at: (0, 0)),
            ],
            scratch_shapes=[pltpu.VMEM((Q, C * width), jnp.bfloat16)],
        ),
        out_shape=(
            jax.ShapeDtypeStruct((pixels, Q), jnp.float32),
            jax.ShapeDtypeStruct((owned, maps), jnp.float32),
        ),
        compiler_params=pltpu.CompilerParams(vmem_limit_bytes=48 * 2**20),
    )(where, left, right, left, left, scale)


def solution(mesh):
    return jax.shard_map(
        shards,
        mesh=mesh,
        in_specs=(P(None, "gr", "gc"), P(None, "gc", None), P(), P()),
        out_specs=(P("gr", "gc"), P(("gr", "gc"), None)),
        check_vma=False,
    )
```

```python
import functools
import math

import jax
import jax.numpy as jnp
from jax import lax
from jax.experimental import pallas as pl
from jax.experimental.pallas import tpu as pltpu
from jax.sharding import PartitionSpec as P

MESH = pl.DeviceIdType.MESH


def sky_kernel(
    G, C, rows, phase_ref, data_ref, ids_ref, table_ref, fisher, maps, left, right, weighted, scale, spare,
    up_sem, down_sem, twin_sem, root_sem, ring_sem, got, got_right,
):
    Z = C // 2
    half, pixels = phase_ref.shape[1:]
    width = 2 * half
    extra = data_ref.shape[0] * data_ref.shape[1]
    Q = right.shape[1]
    owned = pixels // C
    parts = Q // rows
    S = 2 * parts
    g, d = lax.axis_index("gr"), lax.axis_index("gc")
    z, c = d // 2, d % 2
    other = 1 - c
    gy, gx = g // 2, g % 2
    pos = (1 - gx) * gy + gx * (G - 1 - gy)
    ry, rx = z // 2, z % 2
    turn = (pos - ((1 - rx) * ry + rx * (G - 1 - ry)) + G) % G
    is_root = turn == 0

    def ring_device(at):
        at = at % G
        far = at // (G // 2)
        return (1 - far) * 2 * at + far * (2 * (G - 1 - at) + 1)

    ahead, behind = ring_device(pos + 1), ring_device(pos + G - 1)
    send_way = (1 - c) * ahead + c * behind
    not_first, not_last = z > 0, z < Z - 1

    barrier = pltpu.get_barrier_semaphore()

    def greet(device):
        pl.semaphore_signal(barrier, inc=1, device_id=device, device_id_type=MESH)

    greet((g, 2 * z + other))
    for core in range(2):
        greet((ahead, 2 * z + core))
        greet((behind, 2 * z + core))

    @pl.when(not_last)
    def _():
        greet((g, d + 2))

    @pl.when(not_first)
    def _():
        greet((g, d - 2))

    tail = pl.ds(pixels, extra)
    left[d, pl.ds(pixels, half)] = data_ref[0]
    left[d, pl.ds(pixels + half, half)] = data_ref[1]

    pl.semaphore_wait(barrier, 5 + not_last.astype(jnp.int32) + not_first.astype(jnp.int32))

    def remote(src, dst, send_sem, recv_sem, device):
        return pltpu.make_async_remote_copy(
            src_ref=src, dst_ref=dst, send_sem=send_sem, recv_sem=recv_sem, device_id=device, device_id_type=MESH
        )

    def arrived(piece, sem):
        remote(piece, piece, twin_sem.at[0], sem, (g, d)).wait_recv()

    def spread(piece, zb, sem):
        @pl.when((zb <= z) & not_last)
        def _():
            remote(piece, piece, up_sem.at[zb], sem, (g, d + 2)).start()

        @pl.when((zb >= z) & not_first)
        def _():
            remote(piece, piece, down_sem.at[zb], sem, (g, d - 2)).start()

        remote(piece, piece, twin_sem.at[zb], sem, (g, 2 * z + other)).start()

    def start_of(m):
        return pl.multiple_of((m % 2) * Q + (m // 2) * rows, rows)

    def broadcast(piece, zb, block, m):
        at = pl.multiple_of((m // 2) * rows, rows)
        remote(
            piece, right.at[block, pl.ds(at, rows)], root_sem.at[zb], got_right.at[block, m // 2],
            (send_way, 2 * z + m % 2),
        ).start()

    def weights():
        table = jnp.transpose(table_ref[...])
        first = table.astype(jnp.bfloat16)
        rest = table - first.astype(jnp.float32)
        second = rest.astype(jnp.bfloat16)
        third = (rest - second.astype(jnp.float32)).astype(jnp.bfloat16)
        lanes, lines = table.shape
        for b in range(C):
            ids = ids_ref[pl.ds(b, 1)]
            line = lax.broadcasted_iota(jnp.int32, (lines, width), 0)
            pick = (line == ids // lanes).astype(jnp.float32).astype(jnp.bfloat16)
            near = sum(jnp.dot(t, pick, preferred_element_type=jnp.float32) for t in (first, second, third))
            lane = lax.broadcasted_iota(jnp.int32, (lanes, width), 0)
            scale[pl.ds(b, 1)] = jnp.sum(jnp.where(lane == ids % lanes, near, 0.0), axis=0, keepdims=True)

    def scaled(value, b):
        return value.astype(jnp.float32) * scale[pl.ds(b, 1)]

    def prepare(i):
        here = pl.ds(i * rows, rows)

        @pl.when(is_root)
        def _():
            for b in range(C):
                value = scaled(left[b, pl.ds(pl.multiple_of(c * Q + i * rows, rows), rows)], b)
                weighted[b * width:(b + 1) * width, here] = jnp.transpose(value).astype(jnp.bfloat16)

        @pl.when(turn > 0)
        def _():
            for b in range(C):
                value = scaled(right[b, here], b)
                weighted[b * width:(b + 1) * width, here] = jnp.transpose(value).astype(jnp.bfloat16)

    def tile(m, i):
        cut = pl.ds(start_of(m), rows)
        lines = jnp.concatenate([left[b, cut] for b in range(C)], axis=1)
        here = pl.ds(i * rows, rows)
        fisher[cut, here] = jnp.dot(lines, weighted[:, here], preferred_element_type=jnp.float32)

    spread(left.at[d, tail], z, got.at[d, S])
    late = Z + G - 2

    def step(s, carry):
        @pl.when(s < S)
        def _():
            at = start_of(s)
            cut = pl.ds(at, rows)
            value = phase_ref[:, :, cut].reshape(width, rows).astype(jnp.float32)
            left[d, cut] = jnp.transpose(value).astype(jnp.bfloat16)
            spread(left.at[d, cut], z, got.at[d, s])

            @pl.when(is_root)
            def _():
                broadcast(left.at[d, cut], z, d, s)

        for zb in range(Z):
            away = jnp.maximum(zb - z, z - zb)
            mine, twin = 2 * zb + c, 2 * zb + other
            m = s - away

            @pl.when((zb != z) & (m >= 0) & (m < S))
            def _():
                piece = left.at[mine, pl.ds(start_of(m), rows)]
                arrived(piece, got.at[mine, m])
                spread(piece, zb, got.at[mine, m])

                @pl.when(is_root)
                def _():
                    broadcast(piece, zb, mine, m)

            @pl.when((zb != z) & (s == away))
            def _():
                piece = left.at[mine, tail]
                arrived(piece, got.at[mine, S])
                spread(piece, zb, got.at[mine, S])

            n = s - away - 1

            @pl.when((n >= 0) & (n < S))
            def _():
                arrived(left.at[twin, pl.ds(start_of(n), rows)], got.at[twin, n])

            for e in range(2):
                hops = turn if e == 0 else G - turn
                r = s - away - hops

                @pl.when((turn > 0) & (r >= 0) & (r < S) & (r % 2 == c))
                def _():
                    block = 2 * zb + e
                    piece = right.at[block, pl.ds(pl.multiple_of((r // 2) * rows, rows), rows)]
                    arrived(piece, got_right.at[block, r // 2])

                    @pl.when(hops < G - 1)
                    def _():
                        remote(
                            piece, piece, ring_sem.at[block], got_right.at[block, r // 2],
                            (ahead if e == 0 else behind, d),
                        ).start()

        @pl.when(s == 1)
        def _():
            weights()

        for i in range(parts):
            ripe = 2 * i + c + late

            @pl.when(s == ripe)
            def _():
                prepare(i)
                lax.fori_loop(0, jnp.minimum(s - Z, S), lambda m, _: (tile(m, i), 0)[1], 0)

            @pl.when((s >= ripe) & (s >= Z) & (s - Z < S))
            def _():
                tile(s - Z, i)

        @pl.when(s == S + Z - 1)
        def _():
            for zb in range(Z):
                twin = 2 * zb + other
                arrived(left.at[twin, tail], got.at[twin, S])
            skip = d * owned % 16
            cut = pl.ds(pl.multiple_of(d * owned - skip, 16), spare.shape[0])
            mine = jnp.concatenate([scaled(left[b, cut], b).astype(jnp.bfloat16) for b in range(C)], axis=1)
            columns = jnp.concatenate([left[b, tail] for b in range(C)], axis=0)
            spare[...] = jnp.dot(mine, columns, preferred_element_type=jnp.float32)
            maps[...] = spare[pl.ds(pl.multiple_of(skip, 8), owned)]

        return carry

    lax.fori_loop(0, S + late, step, 0)

    def sent(piece, sem):
        remote(piece, piece, sem, got.at[0, 0], (g, d)).wait_send()

    for zb in range(Z):
        mine = 2 * zb + c
        sent(left.at[mine], twin_sem.at[zb])

        @pl.when((zb <= z) & not_last)
        def _():
            sent(left.at[mine], up_sem.at[zb])

        @pl.when((zb >= z) & not_first)
        def _():
            sent(left.at[mine], down_sem.at[zb])

        @pl.when(is_root)
        def _():
            sent(left.at[mine, pl.ds(0, pixels)], root_sem.at[zb])

        for e in range(2):
            block = 2 * zb + e
            hops = turn if e == 0 else G - turn

            @pl.when((turn > 0) & (hops < G - 1))
            def _():
                sent(right.at[block], ring_sem.at[block])


def shards(phase, data, column_ids, noise_weight):
    G, C = lax.axis_size("gr"), lax.axis_size("gc")
    _, pixels, half = phase.shape
    width = 2 * half
    Q = pixels * G // C
    owned = pixels // C
    rows = math.gcd(Q, 256)
    lanes = 128
    tall = owned if owned % 16 == 0 else (owned + 8 + 15) // 16 * 16
    ids = column_ids.reshape(C, half)
    ids = jnp.concatenate([ids, ids], axis=1)
    table = noise_weight.reshape(-1, lanes)
    dma = pltpu.SemaphoreType.DMA
    Z = C // 2
    return pl.pallas_call(
        functools.partial(sky_kernel, G, C, rows),
        out_shape=(
            pltpu.VMEM((pixels, Q), jnp.float32),
            pltpu.VMEM((owned, data.shape[2]), jnp.float32),
        ),
        in_specs=[pl.BlockSpec(memory_space=pltpu.VMEM)] * 4,
        out_specs=(pl.BlockSpec(memory_space=pltpu.VMEM),) * 2,
        scratch_shapes=[
            pltpu.VMEM((C, pixels + width, width), jnp.bfloat16),
            pltpu.VMEM((C, Q, width), jnp.bfloat16),
            pltpu.VMEM((C * width, Q), jnp.bfloat16),
            pltpu.VMEM((C, width), jnp.float32),
            pltpu.VMEM((tall, data.shape[2]), jnp.float32),
            dma((Z,)), dma((Z,)), dma((Z,)), dma((Z,)), dma((C,)),
            dma((C, 2 * (Q // rows) + 1)), dma((C, Q // rows)),
        ],
        compiler_params=pltpu.CompilerParams(
            collective_id=0, has_side_effects=True, vmem_limit_bytes=24 * 2**20
        ),
    )(jnp.transpose(phase, (0, 2, 1)), data, ids, table)


def solution(mesh):
    return jax.shard_map(
        shards,
        mesh=mesh,
        in_specs=(P(None, "gr", "gc"), P(None, "gc", None), P(), P()),
        out_specs=(P("gr", "gc"), P(("gr", "gc"), None)),
        check_vma=False,
    )
```

```python
import functools
import math

import jax
import jax.numpy as jnp
from jax import lax
from jax.experimental import pallas as pl
from jax.experimental.pallas import tpu as pltpu
from jax.sharding import PartitionSpec as P

MESH = pl.DeviceIdType.MESH
ROWS = 128
VMEM_BYTES = 64 * 2**20
SPARE_BYTES = 64 * 2**10


def sky_kernel(
    G, C, rows, group, phase_in, data_in, ids_in, table_in, fisher, maps, phase_ref, data_ref, ids_ref, table_ref,
    left, right, weighted, scale, spare, in_sem, up_sem, down_sem, twin_sem, root_sem, ring_sem, got, got_right,
):
    Z = C // 2
    half, pixels = phase_ref.shape[1:]
    width = 2 * half
    extra = data_ref.shape[0] * data_ref.shape[1]
    Q = right.shape[1]
    owned = pixels // C
    parts = Q // rows
    S = 2 * parts
    g, d = lax.axis_index("gr"), lax.axis_index("gc")
    z, c = d // 2, d % 2
    other = 1 - c
    gy, gx = g // 2, g % 2
    pos = (1 - gx) * gy + gx * (G - 1 - gy)
    ry, rx = z // 2, z % 2
    turn = (pos - ((1 - rx) * ry + rx * (G - 1 - ry)) + G) % G
    is_root = turn == 0

    def ring_device(at):
        at = at % G
        far = at // (G // 2)
        return (1 - far) * 2 * at + far * (2 * (G - 1 - at) + 1)

    ahead, behind = ring_device(pos + 1), ring_device(pos + G - 1)
    send_way = (1 - c) * ahead + c * behind
    not_first, not_last = z > 0, z < Z - 1

    incoming = [
        pltpu.make_async_copy(src, dst, in_sem.at[k])
        for k, (src, dst) in enumerate(
            ((data_in, data_ref), (phase_in, phase_ref), (ids_in, ids_ref), (table_in, table_ref))
        )
    ]
    for copy in incoming:
        copy.start()

    barrier = pltpu.get_barrier_semaphore()

    def greet(device):
        pl.semaphore_signal(barrier, inc=1, device_id=device, device_id_type=MESH)

    greet((g, 2 * z + other))
    for core in range(2):
        greet((ahead, 2 * z + core))
        greet((behind, 2 * z + core))

    @pl.when(not_last)
    def _():
        greet((g, d + 2))

    @pl.when(not_first)
    def _():
        greet((g, d - 2))

    tail = pl.ds(pixels, extra)
    incoming[0].wait()
    left[d, pl.ds(pixels, half)] = data_ref[0]
    left[d, pl.ds(pixels + half, half)] = data_ref[1]

    pl.semaphore_wait(barrier, 5 + not_last.astype(jnp.int32) + not_first.astype(jnp.int32))

    def remote(src, dst, send_sem, recv_sem, device):
        return pltpu.make_async_remote_copy(
            src_ref=src, dst_ref=dst, send_sem=send_sem, recv_sem=recv_sem, device_id=device, device_id_type=MESH
        )

    def arrived(piece, sem):
        remote(piece, piece, twin_sem.at[0], sem, (g, d)).wait_recv()

    def spread(piece, zb, sem):
        @pl.when((zb <= z) & not_last)
        def _():
            remote(piece, piece, up_sem.at[zb], sem, (g, d + 2)).start()

        @pl.when((zb >= z) & not_first)
        def _():
            remote(piece, piece, down_sem.at[zb], sem, (g, d - 2)).start()

        remote(piece, piece, twin_sem.at[zb], sem, (g, 2 * z + other)).start()

    def start_of(m):
        return pl.multiple_of((m % 2) * Q + (m // 2) * rows, rows)

    def broadcast(piece, zb, block, m):
        at = pl.multiple_of((m // 2) * rows, rows)
        remote(
            piece, right.at[block, pl.ds(at, rows)], root_sem.at[zb], got_right.at[block, m // 2],
            (send_way, 2 * z + m % 2),
        ).start()

    def weights():
        table = jnp.transpose(table_ref[...])
        first = table.astype(jnp.bfloat16)
        rest = table - first.astype(jnp.float32)
        second = rest.astype(jnp.bfloat16)
        third = (rest - second.astype(jnp.float32)).astype(jnp.bfloat16)
        lanes, lines = table.shape
        for b in range(0, C, 2):
            ids = ids_ref[pl.ds(b // 2, 1)]
            line = lax.broadcasted_iota(jnp.int32, (lines, width), 0)
            pick = (line == ids // lanes).astype(jnp.float32).astype(jnp.bfloat16)
            near = sum(jnp.dot(t, pick, preferred_element_type=jnp.float32) for t in (first, second, third))
            lane = lax.broadcasted_iota(jnp.int32, (lanes, width), 0)
            both = jnp.sum(jnp.where(lane == ids % lanes, near, 0.0), axis=0, keepdims=True)
            turned = jnp.concatenate([both[:, half:], both[:, :half]], axis=1)
            low = lax.broadcasted_iota(jnp.int32, (1, width), 1) < half
            scale[pl.ds(b, 1)] = jnp.where(low, both, turned)
            scale[pl.ds(b + 1, 1)] = jnp.where(low, turned, both)

    def scaled(value, b):
        return value.astype(jnp.float32) * scale[pl.ds(b, 1)]

    wide = group * rows
    units = parts // group

    def unit_start(u):
        return pl.multiple_of((u % 2) * Q + (u // 2) * wide, wide)

    def prepare(i):
        here = pl.ds(i * wide, wide)

        @pl.when(is_root)
        def _():
            for b in range(C):
                value = scaled(left[b, pl.ds(pl.multiple_of(c * Q + i * wide, wide), wide)], b)
                weighted[b * width:(b + 1) * width, here] = jnp.transpose(value).astype(jnp.bfloat16)

        @pl.when(turn > 0)
        def _():
            for b in range(C):
                value = scaled(right[b, here], b)
                weighted[b * width:(b + 1) * width, here] = jnp.transpose(value).astype(jnp.bfloat16)

    def tile(u, i):
        cut = pl.ds(unit_start(u), wide)
        lines = jnp.concatenate([left[b, cut] for b in range(C)], axis=1)
        here = pl.ds(i * wide, wide)
        fisher[cut, here] = jnp.dot(lines, weighted[:, here], preferred_element_type=jnp.float32)

    spread(left.at[d, tail], z, got.at[d, S])
    for copy in incoming[1:]:
        copy.wait()
    late = Z + G - 2

    def step(s, carry):
        @pl.when(s < S)
        def _():
            at = start_of(s)
            cut = pl.ds(at, rows)
            value = phase_ref[:, :, cut].reshape(width, rows).astype(jnp.float32)
            left[d, cut] = jnp.transpose(value).astype(jnp.bfloat16)
            spread(left.at[d, cut], z, got.at[d, s])

            @pl.when(is_root)
            def _():
                broadcast(left.at[d, cut], z, d, s)

        for zb in range(Z):
            away = jnp.maximum(zb - z, z - zb)
            mine, twin = 2 * zb + c, 2 * zb + other
            m = s - away

            @pl.when((zb != z) & (m >= 0) & (m < S))
            def _():
                piece = left.at[mine, pl.ds(start_of(m), rows)]
                arrived(piece, got.at[mine, m])
                spread(piece, zb, got.at[mine, m])

                @pl.when(is_root)
                def _():
                    broadcast(piece, zb, mine, m)

            @pl.when((zb != z) & (s == away))
            def _():
                piece = left.at[mine, tail]
                arrived(piece, got.at[mine, S])
                spread(piece, zb, got.at[mine, S])

            n = s - away - 1

            @pl.when((n >= 0) & (n < S))
            def _():
                arrived(left.at[twin, pl.ds(start_of(n), rows)], got.at[twin, n])

            for e in range(2):
                hops = turn if e == 0 else G - turn
                r = s - away - hops

                @pl.when((turn > 0) & (r >= 0) & (r < S) & (r % 2 == c))
                def _():
                    block = 2 * zb + e
                    piece = right.at[block, pl.ds(pl.multiple_of((r // 2) * rows, rows), rows)]
                    arrived(piece, got_right.at[block, r // 2])

                    @pl.when(hops < G - 1)
                    def _():
                        remote(
                            piece, piece, ring_sem.at[block], got_right.at[block, r // 2],
                            (ahead if e == 0 else behind, d),
                        ).start()

        @pl.when(s == 1)
        def _():
            weights()

        last = s - Z - 2 * (group - 1)
        cycle = last % (2 * group)
        unit = last // (2 * group) * 2 + cycle
        done = jnp.minimum(last // (2 * group) * 2 + jnp.minimum(cycle, 2), 2 * units)
        for i in range(units):
            ripe = 2 * (group * i + group - 1) + c + late

            @pl.when(s == ripe)
            def _():
                prepare(i)
                lax.fori_loop(0, done, lambda u, _: (tile(u, i), 0)[1], 0)

            @pl.when((s >= ripe) & (last >= 0) & (cycle < 2) & (unit < 2 * units))
            def _():
                tile(unit, i)

        @pl.when(s == S + Z - 1)
        def _():
            for zb in range(Z):
                twin = 2 * zb + other
                arrived(left.at[twin, tail], got.at[twin, S])
            skip = d * owned % 16
            cut = pl.ds(pl.multiple_of(d * owned - skip, 16), spare.shape[0])
            mine = jnp.concatenate([scaled(left[b, cut], b).astype(jnp.bfloat16) for b in range(C)], axis=1)
            columns = jnp.concatenate([left[b, tail] for b in range(C)], axis=0)
            spare[...] = jnp.dot(mine, columns, preferred_element_type=jnp.float32)
            maps[...] = spare[pl.ds(pl.multiple_of(skip, 8), owned)]

        return carry

    lax.fori_loop(0, S + late, step, 0)

    def sent(piece, sem):
        remote(piece, piece, sem, got.at[0, 0], (g, d)).wait_send()

    for zb in range(Z):
        mine = 2 * zb + c
        sent(left.at[mine], twin_sem.at[zb])

        @pl.when((zb <= z) & not_last)
        def _():
            sent(left.at[mine], up_sem.at[zb])

        @pl.when((zb >= z) & not_first)
        def _():
            sent(left.at[mine], down_sem.at[zb])

        @pl.when(is_root)
        def _():
            sent(left.at[mine, pl.ds(0, pixels)], root_sem.at[zb])

        for e in range(2):
            block = 2 * zb + e
            hops = turn if e == 0 else G - turn

            @pl.when((turn > 0) & (hops < G - 1))
            def _():
                sent(right.at[block], ring_sem.at[block])


def shards(phase, data, column_ids, noise_weight):
    G, C = lax.axis_size("gr"), lax.axis_size("gc")
    _, pixels, half = phase.shape
    width = 2 * half
    Q = pixels * G // C
    owned = pixels // C
    wide = math.gcd(Q, 256)
    rows = math.gcd(wide, ROWS)
    lanes = 128
    tall = owned if owned % 16 == 0 else (owned + 8 + 15) // 16 * 16
    ids = column_ids.reshape(C // 2, width)
    table = noise_weight.reshape(-1, lanes)
    dma = pltpu.SemaphoreType.DMA
    Z = C // 2
    return pl.pallas_call(
        functools.partial(sky_kernel, G, C, rows, wide // rows),
        out_shape=(
            pltpu.VMEM((pixels, Q), jnp.float32),
            pltpu.VMEM((owned, data.shape[2]), jnp.float32),
        ),
        in_specs=[pl.BlockSpec(memory_space=pltpu.HBM)] * 4,
        out_specs=(pl.BlockSpec(memory_space=pltpu.VMEM),) * 2,
        scratch_shapes=[
            pltpu.VMEM((2, half, pixels), jnp.bfloat16),
            pltpu.VMEM(data.shape, jnp.bfloat16),
            pltpu.VMEM(ids.shape, jnp.int32),
            pltpu.VMEM(table.shape, jnp.float32),
            pltpu.VMEM((C, pixels + width, width), jnp.bfloat16),
            pltpu.VMEM((C, Q, width), jnp.bfloat16),
            pltpu.VMEM((C * width, Q), jnp.bfloat16),
            pltpu.VMEM((C, width), jnp.float32),
            pltpu.VMEM((tall, data.shape[2]), jnp.float32),
            dma((4,)), dma((Z,)), dma((Z,)), dma((Z,)), dma((Z,)), dma((C,)),
            dma((C, 2 * (Q // rows) + 1)), dma((C, Q // rows)),
        ],
        compiler_params=pltpu.CompilerParams(
            collective_id=0, has_side_effects=True, vmem_limit_bytes=VMEM_BYTES - 4 * (pixels * Q + owned * data.shape[2]) - SPARE_BYTES
        ),
    )(jnp.transpose(phase, (0, 2, 1)), data, ids, table)


def solution(mesh):
    return jax.shard_map(
        shards,
        mesh=mesh,
        in_specs=(P(None, "gr", "gc"), P(None, "gc", None), P(), P()),
        out_specs=(P("gr", "gc"), P(("gr", "gc"), None)),
        check_vma=False,
    )
```

```python
import functools
import math

import jax
import jax.numpy as jnp
from jax import lax
from jax.experimental import pallas as pl
from jax.experimental.pallas import tpu as pltpu
from jax.sharding import PartitionSpec as P

MESH = pl.DeviceIdType.MESH
ROWS = 256
LATE = 2
VMEM_BYTES = 64 * 2**20
SPARE_BYTES = 64 * 2**10


def sky_kernel(
    G, C, rows, group, phase_in, data_in, ids_in, table_in, fisher, left, weighted, scale,
    phase_ref, data_ref, ids_ref, table_ref, right, in_sem, up_sem, down_sem, twin_sem, root_sem, ring_sem, got, got_right,
):
    Z = C // 2
    half, pixels = phase_ref.shape[1:]
    width = 2 * half
    extra = data_ref.shape[0] * data_ref.shape[1]
    Q = right.shape[1]
    parts = Q // rows
    S = 2 * parts
    g, d = lax.axis_index("gr"), lax.axis_index("gc")
    z, c = d // 2, d % 2
    other = 1 - c
    gy, gx = g // 2, g % 2
    pos = (1 - gx) * gy + gx * (G - 1 - gy)
    ry, rx = z // 2, z % 2
    turn = (pos - ((1 - rx) * ry + rx * (G - 1 - ry)) + G) % G
    is_root = turn == 0

    def ring_device(at):
        at = at % G
        far = at // (G // 2)
        return (1 - far) * 2 * at + far * (2 * (G - 1 - at) + 1)

    ahead, behind = ring_device(pos + 1), ring_device(pos + G - 1)
    send_way = (1 - c) * ahead + c * behind
    not_first, not_last = z > 0, z < Z - 1

    incoming = [
        pltpu.make_async_copy(src, dst, in_sem.at[k])
        for k, (src, dst) in enumerate(
            ((data_in, data_ref), (phase_in, phase_ref), (ids_in, ids_ref), (table_in, table_ref))
        )
    ]
    for copy in incoming:
        copy.start()

    barrier = pltpu.get_barrier_semaphore()

    def greet(device):
        pl.semaphore_signal(barrier, inc=1, device_id=device, device_id_type=MESH)

    greet((g, 2 * z + other))
    for core in range(2):
        greet((ahead, 2 * z + core))
        greet((behind, 2 * z + core))

    @pl.when(not_last)
    def _():
        greet((g, d + 2))

    @pl.when(not_first)
    def _():
        greet((g, d - 2))

    tail = pl.ds(pixels, extra)
    incoming[0].wait()
    left[d, pl.ds(pixels, half)] = data_ref[0]
    left[d, pl.ds(pixels + half, half)] = data_ref[1]

    pl.semaphore_wait(barrier, 5 + not_last.astype(jnp.int32) + not_first.astype(jnp.int32))

    def remote(src, dst, send_sem, recv_sem, device):
        return pltpu.make_async_remote_copy(
            src_ref=src, dst_ref=dst, send_sem=send_sem, recv_sem=recv_sem, device_id=device, device_id_type=MESH
        )

    def arrived(piece, sem):
        remote(piece, piece, twin_sem.at[0], sem, (g, d)).wait_recv()

    def spread(piece, zb, sem):
        @pl.when((zb <= z) & not_last)
        def _():
            remote(piece, piece, up_sem.at[zb], sem, (g, d + 2)).start()

        @pl.when((zb >= z) & not_first)
        def _():
            remote(piece, piece, down_sem.at[zb], sem, (g, d - 2)).start()

        remote(piece, piece, twin_sem.at[zb], sem, (g, 2 * z + other)).start()

    def start_of(m):
        return pl.multiple_of((m % 2) * Q + (m // 2) * rows, rows)

    def broadcast(piece, zb, block, m):
        at = pl.multiple_of((m // 2) * rows, rows)
        remote(
            piece, right.at[block, pl.ds(at, rows)], root_sem.at[zb], got_right.at[block, m // 2],
            (send_way, 2 * z + m % 2),
        ).start()

    def weights():
        table = jnp.transpose(table_ref[...])
        first = table.astype(jnp.bfloat16)
        rest = table - first.astype(jnp.float32)
        second = rest.astype(jnp.bfloat16)
        third = (rest - second.astype(jnp.float32)).astype(jnp.bfloat16)
        lanes, lines = table.shape
        for b in range(0, C, 2):
            ids = ids_ref[pl.ds(b // 2, 1)]
            line = lax.broadcasted_iota(jnp.int32, (lines, width), 0)
            pick = (line == ids // lanes).astype(jnp.float32).astype(jnp.bfloat16)
            near = sum(jnp.dot(t, pick, preferred_element_type=jnp.float32) for t in (first, second, third))
            lane = lax.broadcasted_iota(jnp.int32, (lanes, width), 0)
            both = jnp.sum(jnp.where(lane == ids % lanes, near, 0.0), axis=0, keepdims=True)
            turned = jnp.concatenate([both[:, half:], both[:, :half]], axis=1)
            low = lax.broadcasted_iota(jnp.int32, (1, width), 1) < half
            scale[pl.ds(b, 1)] = jnp.where(low, both, turned)
            scale[pl.ds(b + 1, 1)] = jnp.where(low, turned, both)

    def scaled(value, b):
        return value.astype(jnp.float32) * scale[pl.ds(b, 1)]

    wide = group * rows
    units = parts // group
    early = fisher.shape[1] // wide

    def unit_start(u):
        return pl.multiple_of((u % 2) * Q + (u // 2) * wide, wide)

    def prepare(i):
        here = pl.ds(i * wide, wide)

        @pl.when(is_root)
        def _():
            for b in range(C):
                value = scaled(left[b, pl.ds(pl.multiple_of(c * Q + i * wide, wide), wide)], b)
                weighted[b * width:(b + 1) * width, here] = jnp.transpose(value).astype(jnp.bfloat16)

        @pl.when(turn > 0)
        def _():
            for b in range(C):
                value = scaled(right[b, here], b)
                weighted[b * width:(b + 1) * width, here] = jnp.transpose(value).astype(jnp.bfloat16)

    def tile(u, i):
        cut = pl.ds(unit_start(u), wide)
        lines = jnp.concatenate([left[b, cut] for b in range(C)], axis=1)
        here = pl.ds(i * wide, wide)
        fisher[cut, here] = jnp.dot(lines, weighted[:, here], preferred_element_type=jnp.float32)

    spread(left.at[d, tail], z, got.at[d, S])
    for copy in incoming[1:]:
        copy.wait()
    late = Z + G - 2

    def step(s, carry):
        @pl.when(s < S)
        def _():
            at = start_of(s)
            cut = pl.ds(at, rows)
            value = phase_ref[:, :, cut].reshape(width, rows).astype(jnp.float32)
            left[d, cut] = jnp.transpose(value).astype(jnp.bfloat16)
            spread(left.at[d, cut], z, got.at[d, s])

            @pl.when(is_root)
            def _():
                broadcast(left.at[d, cut], z, d, s)

        for zb in range(Z):
            away = jnp.maximum(zb - z, z - zb)
            mine, twin = 2 * zb + c, 2 * zb + other
            m = s - away

            @pl.when((zb != z) & (m >= 0) & (m < S))
            def _():
                piece = left.at[mine, pl.ds(start_of(m), rows)]
                arrived(piece, got.at[mine, m])
                spread(piece, zb, got.at[mine, m])

                @pl.when(is_root)
                def _():
                    broadcast(piece, zb, mine, m)

            @pl.when((zb != z) & (s == away))
            def _():
                piece = left.at[mine, tail]
                arrived(piece, got.at[mine, S])
                spread(piece, zb, got.at[mine, S])

            n = s - away - 1

            @pl.when((n >= 0) & (n < S))
            def _():
                arrived(left.at[twin, pl.ds(start_of(n), rows)], got.at[twin, n])

            for e in range(2):
                hops = turn if e == 0 else G - turn
                r = s - away - hops

                @pl.when((turn > 0) & (r >= 0) & (r < S) & (r % 2 == c))
                def _():
                    block = 2 * zb + e
                    piece = right.at[block, pl.ds(pl.multiple_of((r // 2) * rows, rows), rows)]
                    arrived(piece, got_right.at[block, r // 2])

                    @pl.when(hops < G - 1)
                    def _():
                        remote(
                            piece, piece, ring_sem.at[block], got_right.at[block, r // 2],
                            (ahead if e == 0 else behind, d),
                        ).start()

        @pl.when(s == 1)
        def _():
            weights()

        last = s - Z - 2 * (group - 1)
        cycle = last % (2 * group)
        unit = last // (2 * group) * 2 + cycle
        done = jnp.minimum(last // (2 * group) * 2 + jnp.minimum(cycle, 2), 2 * units)
        for i in range(units):
            ripe = 2 * (group * i + group - 1) + c + late

            @pl.when(s == ripe)
            def _():
                prepare(i)
                if i < early:
                    lax.fori_loop(0, done, lambda u, _: (tile(u, i), 0)[1], 0)

            if i >= early:
                continue

            @pl.when((s >= ripe) & (last >= 0) & (cycle < 2) & (unit < 2 * units))
            def _():
                tile(unit, i)

        @pl.when(s == S + Z - 1)
        def _():
            for zb in range(Z):
                twin = 2 * zb + other
                arrived(left.at[twin, tail], got.at[twin, S])

        return carry

    lax.fori_loop(0, S + late, step, 0)

    def sent(piece, sem):
        remote(piece, piece, sem, got.at[0, 0], (g, d)).wait_send()

    for zb in range(Z):
        mine = 2 * zb + c
        sent(left.at[mine], twin_sem.at[zb])

        @pl.when((zb <= z) & not_last)
        def _():
            sent(left.at[mine], up_sem.at[zb])

        @pl.when((zb >= z) & not_first)
        def _():
            sent(left.at[mine], down_sem.at[zb])

        @pl.when(is_root)
        def _():
            sent(left.at[mine, pl.ds(0, pixels)], root_sem.at[zb])

        for e in range(2):
            block = 2 * zb + e
            hops = turn if e == 0 else G - turn

            @pl.when((turn > 0) & (hops < G - 1))
            def _():
                sent(right.at[block], ring_sem.at[block])


def finish_kernel(C, owned, fisher, left, weighted, scale, out, maps, columns, mine, out_sem, late_sem, maps_sem):
    pixels, early = fisher.shape
    width = left.shape[2]
    step = math.gcd(pixels, 512)
    late = columns.shape[1]
    copy = pltpu.make_async_copy(fisher, out.at[:, pl.ds(0, early)], out_sem)
    copy.start()

    skip = lax.axis_index("gc") * owned % 16
    cut = pl.ds(pl.multiple_of(lax.axis_index("gc") * owned - skip, 16), mine.shape[0])
    rows = [(left[b, cut].astype(jnp.float32) * scale[pl.ds(b, 1)]).astype(jnp.bfloat16) for b in range(C)]
    data = jnp.concatenate([left[b, pl.ds(pixels, width)] for b in range(C)], axis=0)
    mine[...] = jnp.dot(jnp.concatenate(rows, axis=1), data, preferred_element_type=jnp.float32)
    kept = pltpu.make_async_copy(mine.at[pl.ds(pl.multiple_of(skip, 8), owned)], maps, maps_sem)
    kept.start()

    def strip(k):
        part = pl.ds(pl.multiple_of(k * step, step), step)
        return part, pltpu.make_async_copy(columns.at[part], out.at[part, pl.ds(early, late)], late_sem.at[k])

    def multiply(k, carry):
        part, send = strip(k)
        lines = jnp.concatenate([left[b, part] for b in range(C)], axis=1)
        columns[part] = jnp.dot(lines, weighted[:, early:], preferred_element_type=jnp.float32)
        send.start()
        return carry

    lax.fori_loop(0, pixels // step, multiply, 0)
    for k in range(pixels // step):
        strip(k)[1].wait()
    kept.wait()
    copy.wait()


def shards(phase, data, column_ids, noise_weight):
    G, C = lax.axis_size("gr"), lax.axis_size("gc")
    _, pixels, half = phase.shape
    width = 2 * half
    Q = pixels * G // C
    owned = pixels // C
    wide = math.gcd(Q, 256)
    rows = math.gcd(wide, ROWS)
    late = LATE * wide
    lanes = 128
    tall = owned if owned % 16 == 0 else (owned + 8 + 15) // 16 * 16
    ids = column_ids.reshape(C // 2, width)
    table = noise_weight.reshape(-1, lanes)
    dma = pltpu.SemaphoreType.DMA
    Z = C // 2
    held = (
        ((pixels, Q - late), jnp.float32),
        ((C, pixels + width, width), jnp.bfloat16),
        ((C * width, Q), jnp.bfloat16),
        ((C, width), jnp.float32),
    )
    held_bytes = sum(math.prod(shape) * jnp.dtype(kind).itemsize for shape, kind in held)
    kept = pl.pallas_call(
        functools.partial(sky_kernel, G, C, rows, wide // rows),
        out_shape=tuple(pltpu.VMEM(shape, kind) for shape, kind in held),
        in_specs=[pl.BlockSpec(memory_space=pltpu.HBM)] * 4,
        out_specs=(pl.BlockSpec(memory_space=pltpu.VMEM),) * 4,
        scratch_shapes=[
            pltpu.VMEM((2, half, pixels), jnp.bfloat16),
            pltpu.VMEM(data.shape, jnp.bfloat16),
            pltpu.VMEM(ids.shape, jnp.int32),
            pltpu.VMEM(table.shape, jnp.float32),
            pltpu.VMEM((C, Q, width), jnp.bfloat16),
            dma((4,)), dma((Z,)), dma((Z,)), dma((Z,)), dma((Z,)), dma((C,)),
            dma((C, 2 * (Q // rows) + 1)), dma((C, Q // rows)),
        ],
        compiler_params=pltpu.CompilerParams(
            collective_id=0, has_side_effects=True, vmem_limit_bytes=VMEM_BYTES - held_bytes - SPARE_BYTES
        ),
    )(jnp.transpose(phase, (0, 2, 1)), data, ids, table)
    return pl.pallas_call(
        functools.partial(finish_kernel, C, owned),
        out_shape=(
            jax.ShapeDtypeStruct((pixels, Q), jnp.float32),
            jax.ShapeDtypeStruct((owned, data.shape[2]), jnp.float32),
        ),
        in_specs=[pl.BlockSpec(memory_space=pltpu.VMEM)] * 4,
        out_specs=(pl.BlockSpec(memory_space=pltpu.HBM),) * 2,
        scratch_shapes=[
            pltpu.VMEM((pixels, late), jnp.float32),
            pltpu.VMEM((tall, data.shape[2]), jnp.float32),
            dma, dma((pixels // math.gcd(pixels, 512),)), dma,
        ],
        compiler_params=pltpu.CompilerParams(vmem_limit_bytes=12 * 2**20),
    )(*(pltpu.with_memory_space_constraint(array, pltpu.VMEM) for array in kept))


def solution(mesh):
    return jax.shard_map(
        shards,
        mesh=mesh,
        in_specs=(P(None, "gr", "gc"), P(None, "gc", None), P(), P()),
        out_specs=(P("gr", "gc"), P(("gr", "gc"), None)),
        check_vma=False,
    )
```

```python
import functools
import math

import jax
import jax.numpy as jnp
from jax import lax
from jax.experimental import pallas as pl
from jax.experimental.pallas import tpu as pltpu
from jax.sharding import PartitionSpec as P

MESH = pl.DeviceIdType.MESH
ROWS = 256
LATE = 3
VMEM_BYTES = 64 * 2**20
SPARE_BYTES = 64 * 2**10


def sky_kernel(
    G, C, rows, group, phase_in, data_in, ids_in, table_in, fisher, left, weighted, scale,
    phase_ref, data_ref, ids_ref, table_ref, right, in_sem, up_sem, down_sem, twin_sem, root_sem, both_sem, ring_sem, got, got_right,
):
    Z = C // 2
    half, pixels = phase_ref.shape[1:]
    width = 2 * half
    extra = data_ref.shape[0] * data_ref.shape[1]
    Q = right.shape[1]
    parts = Q // rows
    S = 2 * parts
    g, d = lax.axis_index("gr"), lax.axis_index("gc")
    z, c = d // 2, d % 2
    other = 1 - c
    gy, gx = g // 2, g % 2
    pos = (1 - gx) * gy + gx * (G - 1 - gy)
    ry, rx = z // 2, z % 2
    turn = (pos - ((1 - rx) * ry + rx * (G - 1 - ry)) + G) % G
    is_root = turn == 0

    def ring_device(at):
        at = at % G
        far = at // (G // 2)
        return (1 - far) * 2 * at + far * (2 * (G - 1 - at) + 1)

    ahead, behind = ring_device(pos + 1), ring_device(pos + G - 1)
    send_way = (1 - c) * ahead + c * behind
    other_way = c * ahead + (1 - c) * behind
    not_first, not_last = z > 0, z < Z - 1

    incoming = [
        pltpu.make_async_copy(src, dst, in_sem.at[k])
        for k, (src, dst) in enumerate(
            ((data_in, data_ref), (phase_in, phase_ref), (ids_in, ids_ref), (table_in, table_ref))
        )
    ]
    for copy in incoming:
        copy.start()

    barrier = pltpu.get_barrier_semaphore()

    def greet(device):
        pl.semaphore_signal(barrier, inc=1, device_id=device, device_id_type=MESH)

    greet((g, 2 * z + other))
    for core in range(2):
        greet((ahead, 2 * z + core))
        greet((behind, 2 * z + core))

    @pl.when(not_last)
    def _():
        greet((g, d + 2))

    @pl.when(not_first)
    def _():
        greet((g, d - 2))

    tail = pl.ds(pixels, extra)
    incoming[0].wait()
    left[d, pl.ds(pixels, half)] = data_ref[0]
    left[d, pl.ds(pixels + half, half)] = data_ref[1]

    pl.semaphore_wait(barrier, 5 + not_last.astype(jnp.int32) + not_first.astype(jnp.int32))

    def remote(src, dst, send_sem, recv_sem, device):
        return pltpu.make_async_remote_copy(
            src_ref=src, dst_ref=dst, send_sem=send_sem, recv_sem=recv_sem, device_id=device, device_id_type=MESH
        )

    def arrived(piece, sem):
        remote(piece, piece, twin_sem.at[0], sem, (g, d)).wait_recv()

    def spread(piece, zb, sem):
        @pl.when((zb <= z) & not_last)
        def _():
            remote(piece, piece, up_sem.at[zb], sem, (g, d + 2)).start()

        @pl.when((zb >= z) & not_first)
        def _():
            remote(piece, piece, down_sem.at[zb], sem, (g, d - 2)).start()

        remote(piece, piece, twin_sem.at[zb], sem, (g, 2 * z + other)).start()

    def start_of(m):
        return pl.multiple_of((m % 2) * Q + (m // 2) * rows, rows)

    def broadcast(piece, zb, block, m):
        at = pl.multiple_of((m // 2) * rows, rows)
        remote(
            piece, right.at[block, pl.ds(at, rows)], root_sem.at[zb], got_right.at[block, m // 2],
            (send_way, 2 * z + m % 2),
        ).start()

        @pl.when(m >= S - 2)
        def _():
            remote(
                piece, right.at[block, pl.ds(at, rows)], both_sem.at[zb], got_right.at[block, m // 2],
                (other_way, 2 * z + m % 2),
            ).start()

    def weights():
        table = jnp.transpose(table_ref[...])
        first = table.astype(jnp.bfloat16)
        rest = table - first.astype(jnp.float32)
        second = rest.astype(jnp.bfloat16)
        third = (rest - second.astype(jnp.float32)).astype(jnp.bfloat16)
        lanes, lines = table.shape
        for b in range(0, C, 2):
            ids = ids_ref[pl.ds(b // 2, 1)]
            line = lax.broadcasted_iota(jnp.int32, (lines, width), 0)
            pick = (line == ids // lanes).astype(jnp.float32).astype(jnp.bfloat16)
            near = sum(jnp.dot(t, pick, preferred_element_type=jnp.float32) for t in (first, second, third))
            lane = lax.broadcasted_iota(jnp.int32, (lanes, width), 0)
            both = jnp.sum(jnp.where(lane == ids % lanes, near, 0.0), axis=0, keepdims=True)
            turned = jnp.concatenate([both[:, half:], both[:, :half]], axis=1)
            low = lax.broadcasted_iota(jnp.int32, (1, width), 1) < half
            scale[pl.ds(b, 1)] = jnp.where(low, both, turned)
            scale[pl.ds(b + 1, 1)] = jnp.where(low, turned, both)

    def scaled(value, b):
        return value.astype(jnp.float32) * scale[pl.ds(b, 1)]

    wide = group * rows
    units = parts // group
    early = fisher.shape[1] // wide

    def unit_start(u):
        return pl.multiple_of((u % 2) * Q + (u // 2) * wide, wide)

    def prepare(i):
        here = pl.ds(i * wide, wide)

        @pl.when(is_root)
        def _():
            for b in range(C):
                value = scaled(left[b, pl.ds(pl.multiple_of(c * Q + i * wide, wide), wide)], b)
                weighted[b * width:(b + 1) * width, here] = jnp.transpose(value).astype(jnp.bfloat16)

        @pl.when(turn > 0)
        def _():
            for b in range(C):
                value = scaled(right[b, here], b)
                weighted[b * width:(b + 1) * width, here] = jnp.transpose(value).astype(jnp.bfloat16)

    def tile(u, i):
        cut = pl.ds(unit_start(u), wide)
        lines = jnp.concatenate([left[b, cut] for b in range(C)], axis=1)
        here = pl.ds(i * wide, wide)
        fisher[cut, here] = jnp.dot(lines, weighted[:, here], preferred_element_type=jnp.float32)

    spread(left.at[d, tail], z, got.at[d, S])
    for copy in incoming[1:]:
        copy.wait()
    late = Z + G - 2

    def step(s, carry):
        @pl.when(s < S)
        def _():
            at = start_of(s)
            cut = pl.ds(at, rows)
            value = phase_ref[:, :, cut].reshape(width, rows).astype(jnp.float32)
            left[d, cut] = jnp.transpose(value).astype(jnp.bfloat16)
            spread(left.at[d, cut], z, got.at[d, s])

            @pl.when(is_root)
            def _():
                broadcast(left.at[d, cut], z, d, s)

        for zb in range(Z):
            away = jnp.maximum(zb - z, z - zb)
            mine, twin = 2 * zb + c, 2 * zb + other
            m = s - away

            @pl.when((zb != z) & (m >= 0) & (m < S))
            def _():
                piece = left.at[mine, pl.ds(start_of(m), rows)]
                arrived(piece, got.at[mine, m])
                spread(piece, zb, got.at[mine, m])

                @pl.when(is_root)
                def _():
                    broadcast(piece, zb, mine, m)

            @pl.when((zb != z) & (s == away))
            def _():
                piece = left.at[mine, tail]
                arrived(piece, got.at[mine, S])
                spread(piece, zb, got.at[mine, S])

            n = s - away - 1

            @pl.when((n >= 0) & (n < S))
            def _():
                arrived(left.at[twin, pl.ds(start_of(n), rows)], got.at[twin, n])

            for e in range(2):
                hops = turn if e == 0 else G - turn
                block = 2 * zb + e

                def take(r, onward):
                    piece = right.at[block, pl.ds(pl.multiple_of((r // 2) * rows, rows), rows)]
                    arrived(piece, got_right.at[block, r // 2])

                    @pl.when(onward)
                    def _():
                        remote(
                            piece, piece, ring_sem.at[block], got_right.at[block, r // 2],
                            (ahead if e == 0 else behind, d),
                        ).start()

                r = s - away - hops

                @pl.when((turn > 0) & (r >= 0) & (r < S - 2) & (r % 2 == c))
                def _():
                    take(r, hops < G - 1)

                n = s - away - hops + (G - 2) * (hops // (G - 1))

                @pl.when((turn > 0) & (n >= S - 2) & (n < S) & (n % 2 == c))
                def _():
                    take(n, hops < G - 2)

        @pl.when(s == 1)
        def _():
            weights()

        last = s - Z - 2 * (group - 1)
        cycle = last % (2 * group)
        unit = last // (2 * group) * 2 + cycle
        done = jnp.minimum(last // (2 * group) * 2 + jnp.minimum(cycle, 2), 2 * units)
        for i in range(units):
            ripe = 2 * (group * i + group - 1) + c + late - (i == units - 1)

            @pl.when(s == ripe)
            def _():
                prepare(i)
                if i < early:
                    lax.fori_loop(0, done, lambda u, _: (tile(u, i), 0)[1], 0)

            if i >= early:
                continue

            @pl.when((s >= ripe) & (last >= 0) & (cycle < 2) & (unit < 2 * units))
            def _():
                tile(unit, i)

        @pl.when(s == S + Z - 1)
        def _():
            for zb in range(Z):
                twin = 2 * zb + other
                arrived(left.at[twin, tail], got.at[twin, S])

        return carry

    lax.fori_loop(0, S + late - 1, step, 0)

    def sent(piece, sem):
        remote(piece, piece, sem, got.at[0, 0], (g, d)).wait_send()

    for zb in range(Z):
        mine = 2 * zb + c
        sent(left.at[mine], twin_sem.at[zb])

        @pl.when((zb <= z) & not_last)
        def _():
            sent(left.at[mine], up_sem.at[zb])

        @pl.when((zb >= z) & not_first)
        def _():
            sent(left.at[mine], down_sem.at[zb])

        @pl.when(is_root)
        def _():
            sent(left.at[mine, pl.ds(0, pixels)], root_sem.at[zb])
            sent(left.at[mine, pl.ds(0, 2 * rows)], both_sem.at[zb])

        for e in range(2):
            block = 2 * zb + e
            hops = turn if e == 0 else G - turn

            @pl.when((turn > 0) & (hops < G - 2))
            def _():
                sent(right.at[block], ring_sem.at[block])

            @pl.when((turn > 0) & (hops == G - 2))
            def _():
                sent(right.at[block, pl.ds(0, Q - rows)], ring_sem.at[block])


def finish_kernel(C, owned, fisher, left, weighted, scale, out, maps, columns, mine, out_sem, late_sem, maps_sem):
    pixels, early = fisher.shape
    width = left.shape[2]
    step = math.gcd(pixels, 512)
    late = columns.shape[1]
    copy = pltpu.make_async_copy(fisher, out.at[:, pl.ds(0, early)], out_sem)
    copy.start()

    skip = lax.axis_index("gc") * owned % 16
    cut = pl.ds(pl.multiple_of(lax.axis_index("gc") * owned - skip, 16), mine.shape[0])
    rows = [(left[b, cut].astype(jnp.float32) * scale[pl.ds(b, 1)]).astype(jnp.bfloat16) for b in range(C)]
    data = jnp.concatenate([left[b, pl.ds(pixels, width)] for b in range(C)], axis=0)
    mine[...] = jnp.dot(jnp.concatenate(rows, axis=1), data, preferred_element_type=jnp.float32)
    kept = pltpu.make_async_copy(mine.at[pl.ds(pl.multiple_of(skip, 8), owned)], maps, maps_sem)
    kept.start()

    def strip(k):
        part = pl.ds(pl.multiple_of(k * step, step), step)
        return part, pltpu.make_async_copy(columns.at[part], out.at[part, pl.ds(early, late)], late_sem.at[k])

    def multiply(k, carry):
        part, send = strip(k)
        lines = jnp.concatenate([left[b, part] for b in range(C)], axis=1)
        columns[part] = jnp.dot(lines, weighted[:, early:], preferred_element_type=jnp.float32)
        send.start()
        return carry

    lax.fori_loop(0, pixels // step, multiply, 0)
    for k in range(pixels // step):
        strip(k)[1].wait()
    kept.wait()
    copy.wait()


def shards(phase, data, column_ids, noise_weight):
    G, C = lax.axis_size("gr"), lax.axis_size("gc")
    _, pixels, half = phase.shape
    width = 2 * half
    Q = pixels * G // C
    owned = pixels // C
    wide = math.gcd(Q, 256)
    rows = math.gcd(wide, ROWS)
    late = min(LATE, Q // wide - 1) * wide
    lanes = 128
    tall = owned if owned % 16 == 0 else (owned + 8 + 15) // 16 * 16
    ids = column_ids.reshape(C // 2, width)
    table = noise_weight.reshape(-1, lanes)
    dma = pltpu.SemaphoreType.DMA
    Z = C // 2
    held = (
        ((pixels, Q - late), jnp.float32),
        ((C, pixels + width, width), jnp.bfloat16),
        ((C * width, Q), jnp.bfloat16),
        ((C, width), jnp.float32),
    )
    held_bytes = sum(math.prod(shape) * jnp.dtype(kind).itemsize for shape, kind in held)
    kept = pl.pallas_call(
        functools.partial(sky_kernel, G, C, rows, wide // rows),
        out_shape=tuple(pltpu.VMEM(shape, kind) for shape, kind in held),
        in_specs=[pl.BlockSpec(memory_space=pltpu.HBM)] * 4,
        out_specs=(pl.BlockSpec(memory_space=pltpu.VMEM),) * 4,
        scratch_shapes=[
            pltpu.VMEM((2, half, pixels), jnp.bfloat16),
            pltpu.VMEM(data.shape, jnp.bfloat16),
            pltpu.VMEM(ids.shape, jnp.int32),
            pltpu.VMEM(table.shape, jnp.float32),
            pltpu.VMEM((C, Q, width), jnp.bfloat16),
            dma((4,)), dma((Z,)), dma((Z,)), dma((Z,)), dma((Z,)), dma((Z,)), dma((C,)),
            dma((C, 2 * (Q // rows) + 1)), dma((C, Q // rows)),
        ],
        compiler_params=pltpu.CompilerParams(
            collective_id=0, has_side_effects=True, vmem_limit_bytes=VMEM_BYTES - held_bytes - SPARE_BYTES
        ),
    )(jnp.transpose(phase, (0, 2, 1)), data, ids, table)
    return pl.pallas_call(
        functools.partial(finish_kernel, C, owned),
        out_shape=(
            jax.ShapeDtypeStruct((pixels, Q), jnp.float32),
            jax.ShapeDtypeStruct((owned, data.shape[2]), jnp.float32),
        ),
        in_specs=[pl.BlockSpec(memory_space=pltpu.VMEM)] * 4,
        out_specs=(pl.BlockSpec(memory_space=pltpu.HBM),) * 2,
        scratch_shapes=[
            pltpu.VMEM((pixels, late), jnp.float32),
            pltpu.VMEM((tall, data.shape[2]), jnp.float32),
            dma, dma((pixels // math.gcd(pixels, 512),)), dma,
        ],
        compiler_params=pltpu.CompilerParams(vmem_limit_bytes=15 * 2**20),
    )(*(pltpu.with_memory_space_constraint(array, pltpu.VMEM) for array in kept))


def solution(mesh):
    return jax.shard_map(
        shards,
        mesh=mesh,
        in_specs=(P(None, "gr", "gc"), P(None, "gc", None), P(), P()),
        out_specs=(P("gr", "gc"), P(("gr", "gc"), None)),
        check_vma=False,
    )
```

```python
import functools
import math

import jax
import jax.numpy as jnp
from jax import lax
from jax.experimental import pallas as pl
from jax.experimental.pallas import tpu as pltpu
from jax.sharding import PartitionSpec as P

MESH = pl.DeviceIdType.MESH
ROWS = 256
LATE = 3
VMEM_BYTES = 64 * 2**20
SPARE_BYTES = 64 * 2**10


def sky_kernel(
    G, C, rows, group, phase_in, data_in, ids_in, table_in, fisher, left, weighted, scale,
    phase_ref, data_ref, ids_ref, table_ref, right, in_sem, up_sem, down_sem, twin_sem, root_sem, both_sem, ring_sem, got, got_right,
):
    Z = C // 2
    half, pixels = phase_ref.shape[1:]
    width = 2 * half
    extra = data_ref.shape[0] * data_ref.shape[1]
    Q = right.shape[1]
    parts = Q // rows
    S = 2 * parts
    g, d = lax.axis_index("gr"), lax.axis_index("gc")
    z, c = d // 2, d % 2
    other = 1 - c
    gy, gx = g // 2, g % 2
    pos = (1 - gx) * gy + gx * (G - 1 - gy)
    ry, rx = z // 2, z % 2
    turn = (pos - ((1 - rx) * ry + rx * (G - 1 - ry)) + G) % G
    is_root = turn == 0

    def ring_device(at):
        at = at % G
        far = at // (G // 2)
        return (1 - far) * 2 * at + far * (2 * (G - 1 - at) + 1)

    ahead, behind = ring_device(pos + 1), ring_device(pos + G - 1)
    send_way = (1 - c) * ahead + c * behind
    other_way = c * ahead + (1 - c) * behind
    not_first, not_last = z > 0, z < Z - 1

    incoming = [
        pltpu.make_async_copy(src, dst, in_sem.at[k])
        for k, (src, dst) in enumerate(
            ((data_in, data_ref), (phase_in, phase_ref), (ids_in, ids_ref), (table_in, table_ref))
        )
    ]
    for copy in incoming:
        copy.start()

    barrier = pltpu.get_barrier_semaphore()

    def greet(device):
        pl.semaphore_signal(barrier, inc=1, device_id=device, device_id_type=MESH)

    greet((g, 2 * z + other))
    for core in range(2):
        greet((ahead, 2 * z + core))
        greet((behind, 2 * z + core))

    @pl.when(not_last)
    def _():
        greet((g, d + 2))

    @pl.when(not_first)
    def _():
        greet((g, d - 2))

    tail = pl.ds(pixels, extra)
    incoming[0].wait()
    left[d, pl.ds(pixels, half)] = data_ref[0]
    left[d, pl.ds(pixels + half, half)] = data_ref[1]

    pl.semaphore_wait(barrier, 5 + not_last.astype(jnp.int32) + not_first.astype(jnp.int32))

    def remote(src, dst, send_sem, recv_sem, device):
        return pltpu.make_async_remote_copy(
            src_ref=src, dst_ref=dst, send_sem=send_sem, recv_sem=recv_sem, device_id=device, device_id_type=MESH
        )

    def arrived(piece, sem):
        remote(piece, piece, twin_sem.at[0], sem, (g, d)).wait_recv()

    def spread(piece, zb, sem):
        @pl.when((zb <= z) & not_last)
        def _():
            remote(piece, piece, up_sem.at[zb], sem, (g, d + 2)).start()

        @pl.when((zb >= z) & not_first)
        def _():
            remote(piece, piece, down_sem.at[zb], sem, (g, d - 2)).start()

        remote(piece, piece, twin_sem.at[zb], sem, (g, 2 * z + other)).start()

    def start_of(m):
        return pl.multiple_of((m % 2) * Q + (m // 2) * rows, rows)

    def broadcast(piece, zb, block, m):
        at = pl.multiple_of((m // 2) * rows, rows)
        remote(
            piece, right.at[block, pl.ds(at, rows)], root_sem.at[zb], got_right.at[block, m // 2],
            (send_way, 2 * z + m % 2),
        ).start()

        @pl.when(m >= S - 4)
        def _():
            remote(
                piece, right.at[block, pl.ds(at, rows)], both_sem.at[zb], got_right.at[block, m // 2],
                (other_way, 2 * z + m % 2),
            ).start()

    def weights():
        table = jnp.transpose(table_ref[...])
        first = table.astype(jnp.bfloat16)
        rest = table - first.astype(jnp.float32)
        second = rest.astype(jnp.bfloat16)
        third = (rest - second.astype(jnp.float32)).astype(jnp.bfloat16)
        lanes, lines = table.shape
        for b in range(0, C, 2):
            ids = ids_ref[pl.ds(b // 2, 1)]
            line = lax.broadcasted_iota(jnp.int32, (lines, width), 0)
            pick = (line == ids // lanes).astype(jnp.float32).astype(jnp.bfloat16)
            near = sum(jnp.dot(t, pick, preferred_element_type=jnp.float32) for t in (first, second, third))
            lane = lax.broadcasted_iota(jnp.int32, (lanes, width), 0)
            both = jnp.sum(jnp.where(lane == ids % lanes, near, 0.0), axis=0, keepdims=True)
            turned = jnp.concatenate([both[:, half:], both[:, :half]], axis=1)
            low = lax.broadcasted_iota(jnp.int32, (1, width), 1) < half
            scale[pl.ds(b, 1)] = jnp.where(low, both, turned)
            scale[pl.ds(b + 1, 1)] = jnp.where(low, turned, both)

    def scaled(value, b):
        return value.astype(jnp.float32) * scale[pl.ds(b, 1)]

    wide = group * rows
    units = parts // group
    early = fisher.shape[1] // wide

    def unit_start(u):
        return pl.multiple_of((u % 2) * Q + (u // 2) * wide, wide)

    def prepare(i):
        here = pl.ds(i * wide, wide)

        @pl.when(is_root)
        def _():
            for b in range(C):
                value = scaled(left[b, pl.ds(pl.multiple_of(c * Q + i * wide, wide), wide)], b)
                weighted[b * width:(b + 1) * width, here] = jnp.transpose(value).astype(jnp.bfloat16)

        @pl.when(turn > 0)
        def _():
            for b in range(C):
                value = scaled(right[b, here], b)
                weighted[b * width:(b + 1) * width, here] = jnp.transpose(value).astype(jnp.bfloat16)

    def tile(u, i):
        cut = pl.ds(unit_start(u), wide)
        lines = jnp.concatenate([left[b, cut] for b in range(C)], axis=1)
        here = pl.ds(i * wide, wide)
        fisher[cut, here] = jnp.dot(lines, weighted[:, here], preferred_element_type=jnp.float32)

    spread(left.at[d, tail], z, got.at[d, S])
    for copy in incoming[1:]:
        copy.wait()
    late = Z + G - 2

    def step(s, carry):
        @pl.when(s < S)
        def _():
            at = start_of(s)
            cut = pl.ds(at, rows)
            value = phase_ref[:, :, cut].reshape(width, rows).astype(jnp.float32)
            left[d, cut] = jnp.transpose(value).astype(jnp.bfloat16)
            spread(left.at[d, cut], z, got.at[d, s])

            @pl.when(is_root)
            def _():
                broadcast(left.at[d, cut], z, d, s)

        for zb in range(Z):
            away = jnp.maximum(zb - z, z - zb)
            mine, twin = 2 * zb + c, 2 * zb + other
            m = s - away

            @pl.when((zb != z) & (m >= 0) & (m < S))
            def _():
                piece = left.at[mine, pl.ds(start_of(m), rows)]
                arrived(piece, got.at[mine, m])
                spread(piece, zb, got.at[mine, m])

                @pl.when(is_root)
                def _():
                    broadcast(piece, zb, mine, m)

            @pl.when((zb != z) & (s == away))
            def _():
                piece = left.at[mine, tail]
                arrived(piece, got.at[mine, S])
                spread(piece, zb, got.at[mine, S])

            n = s - away - 1

            @pl.when((n >= 0) & (n < S))
            def _():
                arrived(left.at[twin, pl.ds(start_of(n), rows)], got.at[twin, n])

            for e in range(2):
                hops = turn if e == 0 else G - turn
                block = 2 * zb + e

                def take(r, onward):
                    piece = right.at[block, pl.ds(pl.multiple_of((r // 2) * rows, rows), rows)]
                    arrived(piece, got_right.at[block, r // 2])

                    @pl.when(onward)
                    def _():
                        remote(
                            piece, piece, ring_sem.at[block], got_right.at[block, r // 2],
                            (ahead if e == 0 else behind, d),
                        ).start()

                r = s - away - hops

                @pl.when((turn > 0) & (r >= 0) & (r < S - 4) & (r % 2 == c))
                def _():
                    take(r, hops < G - 1)

                n = s - away - hops + (G - 2) * (hops // (G - 1))

                @pl.when((turn > 0) & (n >= S - 4) & (n < S) & (n % 2 == c))
                def _():
                    take(n, hops < G - 2)

        @pl.when(s == 1)
        def _():
            weights()

        last = s - Z - 2 * (group - 1)
        cycle = last % (2 * group)
        unit = last // (2 * group) * 2 + cycle
        done = jnp.minimum(last // (2 * group) * 2 + jnp.minimum(cycle, 2), 2 * units)
        for i in range(units):
            ripe = 2 * (group * i + group - 1) + c + late - (i >= units - 2)

            @pl.when(s == ripe)
            def _():
                prepare(i)
                if i < early:
                    lax.fori_loop(0, done, lambda u, _: (tile(u, i), 0)[1], 0)

            if i >= early:
                continue

            @pl.when((s >= ripe) & (last >= 0) & (cycle < 2) & (unit < 2 * units))
            def _():
                tile(unit, i)

        @pl.when(s == S + Z - 1)
        def _():
            for zb in range(Z):
                twin = 2 * zb + other
                arrived(left.at[twin, tail], got.at[twin, S])

        return carry

    lax.fori_loop(0, S + late - 1, step, 0)

    def sent(piece, sem):
        remote(piece, piece, sem, got.at[0, 0], (g, d)).wait_send()

    for zb in range(Z):
        mine = 2 * zb + c
        sent(left.at[mine], twin_sem.at[zb])

        @pl.when((zb <= z) & not_last)
        def _():
            sent(left.at[mine], up_sem.at[zb])

        @pl.when((zb >= z) & not_first)
        def _():
            sent(left.at[mine], down_sem.at[zb])

        @pl.when(is_root)
        def _():
            sent(left.at[mine, pl.ds(0, pixels)], root_sem.at[zb])
            sent(left.at[mine, pl.ds(0, 4 * rows)], both_sem.at[zb])

        for e in range(2):
            block = 2 * zb + e
            hops = turn if e == 0 else G - turn

            @pl.when((turn > 0) & (hops < G - 2))
            def _():
                sent(right.at[block], ring_sem.at[block])

            @pl.when((turn > 0) & (hops == G - 2))
            def _():
                sent(right.at[block, pl.ds(0, Q - 2 * rows)], ring_sem.at[block])


def finish_kernel(C, owned, fisher, left, weighted, scale, out, maps, columns, mine, out_sem, late_sem, maps_sem):
    pixels, early = fisher.shape
    width = left.shape[2]
    step = math.gcd(pixels, 512)
    late = columns.shape[1]
    copy = pltpu.make_async_copy(fisher, out.at[:, pl.ds(0, early)], out_sem)
    copy.start()

    skip = lax.axis_index("gc") * owned % 16
    cut = pl.ds(pl.multiple_of(lax.axis_index("gc") * owned - skip, 16), mine.shape[0])
    rows = [(left[b, cut].astype(jnp.float32) * scale[pl.ds(b, 1)]).astype(jnp.bfloat16) for b in range(C)]
    data = jnp.concatenate([left[b, pl.ds(pixels, width)] for b in range(C)], axis=0)
    mine[...] = jnp.dot(jnp.concatenate(rows, axis=1), data, preferred_element_type=jnp.float32)
    kept = pltpu.make_async_copy(mine.at[pl.ds(pl.multiple_of(skip, 8), owned)], maps, maps_sem)
    kept.start()

    def strip(k):
        part = pl.ds(pl.multiple_of(k * step, step), step)
        return part, pltpu.make_async_copy(columns.at[part], out.at[part, pl.ds(early, late)], late_sem.at[k])

    def multiply(k, carry):
        part, send = strip(k)
        lines = jnp.concatenate([left[b, part] for b in range(C)], axis=1)
        columns[part] = jnp.dot(lines, weighted[:, early:], preferred_element_type=jnp.float32)
        send.start()
        return carry

    lax.fori_loop(0, pixels // step, multiply, 0)
    for k in range(pixels // step):
        strip(k)[1].wait()
    kept.wait()
    copy.wait()


def shards(phase, data, column_ids, noise_weight):
    G, C = lax.axis_size("gr"), lax.axis_size("gc")
    _, pixels, half = phase.shape
    width = 2 * half
    Q = pixels * G // C
    owned = pixels // C
    wide = math.gcd(Q, 256)
    rows = math.gcd(wide, ROWS)
    late = min(LATE, Q // wide - 1) * wide
    lanes = 128
    tall = owned if owned % 16 == 0 else (owned + 8 + 15) // 16 * 16
    ids = column_ids.reshape(C // 2, width)
    table = noise_weight.reshape(-1, lanes)
    dma = pltpu.SemaphoreType.DMA
    Z = C // 2
    held = (
        ((pixels, Q - late), jnp.float32),
        ((C, pixels + width, width), jnp.bfloat16),
        ((C * width, Q), jnp.bfloat16),
        ((C, width), jnp.float32),
    )
    held_bytes = sum(math.prod(shape) * jnp.dtype(kind).itemsize for shape, kind in held)
    kept = pl.pallas_call(
        functools.partial(sky_kernel, G, C, rows, wide // rows),
        out_shape=tuple(pltpu.VMEM(shape, kind) for shape, kind in held),
        in_specs=[pl.BlockSpec(memory_space=pltpu.HBM)] * 4,
        out_specs=(pl.BlockSpec(memory_space=pltpu.VMEM),) * 4,
        scratch_shapes=[
            pltpu.VMEM((2, half, pixels), jnp.bfloat16),
            pltpu.VMEM(data.shape, jnp.bfloat16),
            pltpu.VMEM(ids.shape, jnp.int32),
            pltpu.VMEM(table.shape, jnp.float32),
            pltpu.VMEM((C, Q, width), jnp.bfloat16),
            dma((4,)), dma((Z,)), dma((Z,)), dma((Z,)), dma((Z,)), dma((Z,)), dma((C,)),
            dma((C, 2 * (Q // rows) + 1)), dma((C, Q // rows)),
        ],
        compiler_params=pltpu.CompilerParams(
            collective_id=0, has_side_effects=True, vmem_limit_bytes=VMEM_BYTES - held_bytes - SPARE_BYTES
        ),
    )(jnp.transpose(phase, (0, 2, 1)), data, ids, table)
    return pl.pallas_call(
        functools.partial(finish_kernel, C, owned),
        out_shape=(
            jax.ShapeDtypeStruct((pixels, Q), jnp.float32),
            jax.ShapeDtypeStruct((owned, data.shape[2]), jnp.float32),
        ),
        in_specs=[pl.BlockSpec(memory_space=pltpu.VMEM)] * 4,
        out_specs=(pl.BlockSpec(memory_space=pltpu.HBM),) * 2,
        scratch_shapes=[
            pltpu.VMEM((pixels, late), jnp.float32),
            pltpu.VMEM((tall, data.shape[2]), jnp.float32),
            dma, dma((pixels // math.gcd(pixels, 512),)), dma,
        ],
        compiler_params=pltpu.CompilerParams(vmem_limit_bytes=15 * 2**20),
    )(*(pltpu.with_memory_space_constraint(array, pltpu.VMEM) for array in kept))


def solution(mesh):
    return jax.shard_map(
        shards,
        mesh=mesh,
        in_specs=(P(None, "gr", "gc"), P(None, "gc", None), P(), P()),
        out_specs=(P("gr", "gc"), P(("gr", "gc"), None)),
        check_vma=False,
    )
```
